32 devices in a mesh: shard: 4 (over y, x), ctx: 4 (over z), tp: 2 (over core).
Axes of the slice: x: 2, y: 2, z: 4, core: 2. Of those that a mesh axis runs over, the one named last changes fastest.
Arguments:
- tokens: bfloat16 [8192, 1024], P(('shard', 'ctx')), may hold values from -6 to 6
- segment: int32 [8192], P('shard'), may hold values from 0 to 4, as said below
- gain_attn: bfloat16 [1024], P('shard'), may hold values from 0.5 to 1.5
- w_query: bfloat16 [1024, 512], P('shard', 'tp'), may hold values from -0.1875 to 0.1875
- key_value_weight: bfloat16 [1024, 256], P('shard', 'tp'), may hold values from -0.1875 to 0.1875
- w_attn_out: bfloat16 [512, 1024], P('tp', 'shard'), may hold values from -1 to 1
- w_gate_z: bfloat16 [1024, 1536], P('shard', 'tp'), may hold values from -0.1875 to 0.1875
- w_ssm_in: bfloat16 [1024, 1536], P('shard', 'tp'), may hold values from -0.1875 to 0.1875
- w_step: bfloat16 [1024, 24], P('shard', 'tp'), may hold values from -0.1875 to 0.1875
- w_bc: bfloat16 [1024, 256], P('shard'), may hold values from -0.1875 to 0.1875
- w_conv_x: float32 [4, 1536], P(None, 'tp'), may hold values from -0.5 to 0.5
- conv_x_bias: float32 [1536], P('tp'), may hold values from -0.5 to 0.5
- w_conv_bc: float32 [4, 256], replicated, may hold values from -0.5 to 0.5
- conv_bc_bias: float32 [256], replicated, may hold values from -0.5 to 0.5
- step_bias: float32 [24], P('tp'), may hold values from -4 to -1
- decay_log: float32 [24], P('tp'), may hold values from -7 to -1.5
- skip_gain: float32 [24], P('tp'), may hold values from 0.5 to 1.5
- w_ssm_out: bfloat16 [1536, 1024], P('tp', 'shard'), may hold values from -0.01953125 to 0.01953125
- gain_ffn: bfloat16 [1024], P('shard'), may hold values from 0.5 to 1.5
- w_gate: bfloat16 [1024, 2048], P('shard', 'tp'), may hold values from -0.1875 to 0.1875
- w_up: bfloat16 [1024, 2048], P('shard', 'tp'), may hold values from -0.1875 to 0.1875
- w_down: bfloat16 [2048, 1024], P('tp', 'shard'), may hold values from -0.125 to 0.125
- grad_out: bfloat16 [8192, 1024], P(('shard', 'ctx')), may hold values from -6 to 6
Outputs:
- result: bfloat16 [8192, 1024], P(('shard', 'ctx'))
- grad_tokens: bfloat16 [8192, 1024], P(('shard', 'ctx'))
- grad_gain_attn: float32 [1024], P('shard')
- grad_w_query: float32 [1024, 512], P('shard', 'tp')
- grad_w_keyval: float32 [1024, 256], P('shard', 'tp')
- grad_w_attn_out: float32 [512, 1024], P('tp', 'shard')
- grad_w_gate_z: float32 [1024, 1536], P('shard', 'tp')
- grad_w_ssm_in: float32 [1024, 1536], P('shard', 'tp')
- grad_w_step: float32 [1024, 24], P('shard', 'tp')
- grad_w_bc: float32 [1024, 256], P('shard')
- grad_w_conv_x: float32 [4, 1536], P(None, 'tp')
- grad_conv_x_bias: float32 [1536], P('tp')
- grad_w_conv_bc: float32 [4, 256], replicated
- grad_conv_bc_bias: float32 [256], replicated
- grad_step_bias: float32 [24], P('tp')
- grad_decay_log: float32 [24], P('tp')
- grad_skip_gain: float32 [24], P('tp')
- grad_w_ssm_out: float32 [1536, 1024], P('tp', 'shard')
- grad_gain_ffn: float32 [1024], P('shard')
- grad_w_gate: float32 [1024, 2048], P('shard', 'tp')
- grad_w_up: float32 [1024, 2048], P('shard', 'tp')
- grad_w_down: float32 [2048, 1024], P('tp', 'shard')
The draws below stay inside these ranges and needn't reach their ends.
Inputs may be any that keep to these rules, and one draw needn't show every extreme that they name: `segment`: within each aligned run of 2048 tokens (one group) the numbers never fall and the last token has 4; one sequence of each group has 64 or more tokens among the group's first 512 and among its last 512.
All inputs are finite; a program needn't handle non-finite values.
Results may differ from the reference program's by a relative error of at most 0.024.
Values may be sent and summed in bfloat16 or wider, within the bound.
A program may use at most 192 MiB of HBM per device.

```python
from functools import partial
import jax
import jax.numpy as jnp
from jax import lax

MODEL_WIDTH = 1024
QUERY_HEADS = 8
KEY_VALUE_HEADS = 2
HEAD_SIZE = 64
MH = 24
MP = 64
NS = 128
FF = 2048
SPAN = 128
TAPS = 4
TOK_DEV = 512
EDGE = 64
DS = 1536
TOKENS = 8192
N_CTX = 4


def draw_segment(key, part):
    key = jax.random.fold_in(key, 11)
    group_size = TOK_DEV * N_CTX
    groups = TOKENS // group_size
    key_begin, key_finish, key_before, key_after = jax.random.split(key, 4)
    begin = jax.random.randint(key_begin, (groups, 1), 0, TOK_DEV - EDGE + 1)
    finish = group_size - 1 - jax.random.randint(key_finish, (groups, 1), 0, TOK_DEV - EDGE)
    before = jax.random.randint(key_before, (groups, 1), 0, begin + 1)
    after = finish + jax.random.randint(key_after, (groups, 1), 0, group_size - finish)
    position = jnp.arange(group_size)[None, :]
    ids = (position >= before).astype(jnp.int32) + (position >= begin).astype(jnp.int32)
    ids = ids + (position >= finish).astype(jnp.int32) + (position >= after).astype(jnp.int32)
    return ids.reshape(-1)


def levels(stream_key, dims, shards, smallest, top_value):
    def one(dim, blocks):
        heights = jax.random.uniform(jax.random.fold_in(jax.random.fold_in(stream_key, 6), dim), (blocks,), jnp.float32, smallest / len(shards), top_value / len(shards))
        return jnp.repeat(jnp.exp(heights), dims[dim] // blocks).reshape((-1,) + (1,) * (len(dims) - dim - 1))

    factor_of = one(*shards[0])
    for cut in shards[1:]:
        factor_of = factor_of * one(*cut)
    return factor_of


def noise(own_key, shape, width, bound, cuts=(), held_as=jnp.bfloat16):
    values = width * jax.random.normal(own_key, shape, jnp.float32)
    if cuts:
        values = values * levels(own_key, shape, cuts, -0.22, 0.18)
    return jnp.clip(values, -bound, bound).astype(held_as)


def setup_inputs(seed: int = 0) -> dict:
    seeds = jax.random.split(jax.random.key(seed), 24)
    return {
        "tokens": noise(seeds[0], (TOKENS, MODEL_WIDTH), 1.0, 6.0, ((0, 16),)),
        "segment": draw_segment(jax.random.fold_in(seeds[23], 71), 0),
        "gain_attn": jnp.clip(1.0 + 0.1 * jax.random.normal(seeds[2], (MODEL_WIDTH,), jnp.float32), 0.5, 1.5).astype(jnp.bfloat16),
        "w_query": noise(seeds[3], (MODEL_WIDTH, QUERY_HEADS * HEAD_SIZE), MODEL_WIDTH ** -0.5, 0.1875, ((0, 4), (1, 2))),
        "key_value_weight": noise(seeds[4], (MODEL_WIDTH, 2 * KEY_VALUE_HEADS * HEAD_SIZE), MODEL_WIDTH ** -0.5, 0.1875, ((0, 4), (1, 2))),
        "w_attn_out": noise(seeds[5], (QUERY_HEADS * HEAD_SIZE, MODEL_WIDTH), (QUERY_HEADS * HEAD_SIZE // 16) ** -0.5, 1.0, ((0, 2), (1, 4))),
        "w_gate_z": noise(seeds[6], (MODEL_WIDTH, DS), MODEL_WIDTH ** -0.5, 0.1875, ((0, 4), (1, 2))),
        "w_ssm_in": noise(seeds[7], (MODEL_WIDTH, DS), MODEL_WIDTH ** -0.5, 0.1875, ((0, 4), (1, 2))),
        "w_step": noise(seeds[8], (MODEL_WIDTH, MH), MODEL_WIDTH ** -0.5, 0.1875, ((0, 4), (1, 2))),
        "w_bc": noise(seeds[9], (MODEL_WIDTH, 2 * NS), MODEL_WIDTH ** -0.5, 0.1875, ((0, 4),)),
        "w_conv_x": jnp.clip(jax.random.uniform(seeds[10], (TAPS, DS), jnp.float32, -0.5, 0.5) * levels(seeds[10], (TAPS, DS), ((1, 2),), -0.4, 0.0), -0.5, 0.5),
        "conv_x_bias": jnp.clip(jax.random.uniform(seeds[11], (DS,), jnp.float32, -0.5, 0.5) * levels(seeds[11], (DS,), ((0, 2),), -0.4, 0.0), -0.5, 0.5),
        "w_conv_bc": jnp.clip(jax.random.uniform(seeds[12], (TAPS, 2 * NS), jnp.float32, -0.5, 0.5), -0.5, 0.5),
        "conv_bc_bias": jnp.clip(jax.random.uniform(seeds[13], (2 * NS,), jnp.float32, -0.5, 0.5), -0.5, 0.5),
        "step_bias": jnp.clip(-4.0 + 3.0 * jax.random.uniform(seeds[14], (MH,), jnp.float32) ** levels(seeds[14], (MH,), ((0, 2),), -0.2, 0.2), -4.0, -1.0),
        "decay_log": jnp.clip(-7.0 + 5.5 * jax.random.uniform(seeds[15], (MH,), jnp.float32) ** levels(seeds[15], (MH,), ((0, 2),), -0.2, 0.2), -7.0, -1.5),
        "skip_gain": jnp.clip(0.5 + 1.0 * jax.random.uniform(seeds[16], (MH,), jnp.float32) ** levels(seeds[16], (MH,), ((0, 2),), -0.2, 0.2), 0.5, 1.5),
        "w_ssm_out": noise(seeds[17], (DS, MODEL_WIDTH), (DS * 64) ** -0.5, 0.01953125, ((0, 2), (1, 4))),
        "gain_ffn": jnp.clip(1.0 + 0.1 * jax.random.normal(seeds[18], (MODEL_WIDTH,), jnp.float32), 0.5, 1.5).astype(jnp.bfloat16),
        "w_gate": noise(seeds[19], (MODEL_WIDTH, FF), MODEL_WIDTH ** -0.5, 0.1875, ((0, 4), (1, 2))),
        "w_up": noise(seeds[20], (MODEL_WIDTH, FF), MODEL_WIDTH ** -0.5, 0.1875, ((0, 4), (1, 2))),
        "w_down": noise(seeds[21], (FF, MODEL_WIDTH), FF ** -0.5, 0.125, ((0, 2), (1, 4))),
        "grad_out": noise(seeds[22], (TOKENS, MODEL_WIDTH), 1.0, 6.0, ((0, 16),)),
    }


@jax.custom_vjp
def reduced_precision(v):
    return lax.optimization_barrier(v.astype(jnp.bfloat16)).astype(jnp.float32)

@jax.custom_vjp
def reduced_precision_backward(v):
    return v

def low_keep(v):
    return (reduced_precision(v), None)

def low_pass(kept, grad):
    return (grad,)

def back_keep(v):
    return (v, None)

def back_low(kept, grad):
    return (reduced_precision(grad),)
reduced_precision.defvjp(low_keep, low_pass)
reduced_precision_backward.defvjp(back_keep, back_low)
HIGHEST = lax.Precision.HIGHEST
ROPE_BASE = 100000000000.0

def accurate_product(former, latter):
    return jnp.dot(former, latter, precision=HIGHEST, preferred_element_type=jnp.float32)

def rms_scale(values):
    return lax.rsqrt(lax.optimization_barrier(jnp.mean(values * values, axis=-1, keepdims=True)) + 1e-05)

def positions_in_group(segments):
    count = segments.shape[0]
    index = jnp.arange(count, dtype=jnp.int32)
    fresh = jnp.concatenate([jnp.ones((1,), bool), segments[1:] != segments[:-1]])
    starts = lax.cummax(jnp.where(fresh, index, 0).astype(jnp.int32), axis=0)
    return index - starts

def rope_tables(positions):
    exponents = jnp.arange(0, HEAD_SIZE, 2, dtype=jnp.float32) / HEAD_SIZE
    frequency = ROPE_BASE ** (-exponents)
    angle = positions.astype(jnp.float32)[:, None] * frequency[None, :]
    cosine = jnp.cos(angle)
    sine = jnp.sin(angle)
    return (jnp.concatenate([cosine, cosine], axis=-1), jnp.concatenate([sine, sine], axis=-1))

def rotate(values, cosine, sine):
    half = values.shape[-1] // 2
    turned = jnp.concatenate([-values[..., half:], values[..., :half]], axis=-1)
    return values * cosine + turned * sine

def conv_silu(extended, taps, bias, seg_ext):
    reach = taps.shape[0] - 1
    packed_length = extended.shape[0] - reach
    current = seg_ext[reach:]
    total = jnp.zeros((packed_length, extended.shape[1]), jnp.float32) + bias[None, :]
    for delay in range(taps.shape[0]):
        source = extended[reach - delay:reach - delay + packed_length]
        same = (seg_ext[reach - delay:reach - delay + packed_length] == current)[:, None]
        total = total + jnp.where(same, taps[delay][None, :] * source, 0.0)
    return jax.nn.silu(total)

def span_step(decay_rates, carried, block_in):
    states, seg_last = carried
    x_block, b_block, c_block, step_block, seg_block = block_in
    cumulative = jnp.cumsum(step_block * decay_rates[None, :], axis=0)
    packed_length = seg_block.shape[0]
    position = jnp.arange(packed_length)
    causal = (position[:, None] >= position[None, :]) & (seg_block[:, None] == seg_block[None, :])
    spread = cumulative[:, None, :] - cumulative[None, :, :]
    decays = jnp.where(causal[:, :, None], jnp.exp(jnp.minimum(spread, 0.0)), 0.0)
    intersection = jnp.dot(c_block, b_block.T, precision=HIGHEST)
    weighted = intersection[:, :, None] * decays
    inflow = step_block[:, :, None] * x_block
    outputs = jnp.einsum('tuh,uhp->thp', weighted, inflow, precision=HIGHEST)
    carry_in = jnp.where((seg_block == seg_last)[:, None], jnp.exp(cumulative), 0.0)
    outputs = outputs + carry_in[:, :, None] * jnp.einsum('tn,hpn->thp', c_block, states, precision=HIGHEST)
    ending = jnp.where((seg_block == seg_block[-1])[:, None], jnp.exp(cumulative[-1][None, :] - cumulative), 0.0)
    keep_all = jnp.where(seg_block[-1] == seg_last, jnp.exp(cumulative[-1]), 0.0)
    states = keep_all[:, None, None] * states + jnp.einsum('uh,uhp,un->hpn', ending, inflow, b_block, precision=HIGHEST)
    return ((states, seg_block[-1]), outputs)

def ssm_group(inputs, b_values, c_values, steps, decay_log, segments):
    packed_length = inputs.shape[0]
    blocks = packed_length // SPAN
    head_count = decay_log.shape[0]

    def to_blocks(values):
        return values.reshape((blocks, SPAN) + values.shape[1:])
    initial = (jnp.zeros((head_count, MP, NS), jnp.float32), jnp.array(-1, jnp.int32))
    stepper = jax.checkpoint(partial(span_step, -jnp.exp(decay_log)))
    final_state, outputs = lax.scan(stepper, initial, (to_blocks(inputs), to_blocks(b_values), to_blocks(c_values), to_blocks(steps), to_blocks(segments)))
    return outputs.reshape(inputs.shape)

def attend(queries, key_value_rows, segments):
    packed_length = queries.shape[0]
    query_heads = queries.reshape(packed_length, QUERY_HEADS, HEAD_SIZE).transpose(1, 0, 2)
    key_value_pair = key_value_rows.reshape(packed_length, KEY_VALUE_HEADS, 2, HEAD_SIZE)
    per_head_keys = jnp.repeat(key_value_pair[:, :, 0].transpose(1, 0, 2), QUERY_HEADS // KEY_VALUE_HEADS, axis=0)
    per_head_values = jnp.repeat(key_value_pair[:, :, 1].transpose(1, 0, 2), QUERY_HEADS // KEY_VALUE_HEADS, axis=0)
    position = jnp.arange(packed_length)
    allowed = (position[:, None] >= position[None, :]) & (segments[:, None] == segments[None, :])

    def one_head(operands):
        query_one, key_one, value_one = operands
        scores = reduced_precision_backward(accurate_product(query_one, key_one.T) * HEAD_SIZE ** (-0.5))
        scores = jnp.where(allowed, scores, -1e+30)
        row_peak = lax.optimization_barrier(jnp.max(scores, axis=-1, keepdims=True))
        expon = jnp.where(allowed, jnp.exp(scores - row_peak), 0.0)
        weights_soft = expon / lax.optimization_barrier(jnp.sum(expon, axis=-1, keepdims=True))
        return accurate_product(weights_soft, value_one)
    outputs = lax.map(jax.checkpoint(one_head), (query_heads, per_head_keys, per_head_values))
    return outputs.transpose(1, 0, 2).reshape(packed_length, QUERY_HEADS * HEAD_SIZE)

def layer(params, hidden_in, segments):
    gain_attn, w_query, key_value_weight, w_attn_out, w_gate_z, w_ssm_in, w_step, w_bc, w_conv_x, conv_x_bias, w_conv_bc, conv_bc_bias, step_bias, decay_log, skip_gain, w_ssm_out, gain_ffn, w_gate, w_up, w_down = params
    packed_length = hidden_in.shape[0]
    cosine, sine = rope_tables(positions_in_group(segments))
    normalized_input = reduced_precision(hidden_in * rms_scale(hidden_in) * gain_attn)
    query_raw = reduced_precision_backward(accurate_product(normalized_input, w_query)).reshape(packed_length, QUERY_HEADS, HEAD_SIZE)
    queries = reduced_precision(rotate(query_raw, cosine[:, None, :], sine[:, None, :]).reshape(packed_length, QUERY_HEADS * HEAD_SIZE))
    unrotated_key_value = reduced_precision_backward(accurate_product(normalized_input, key_value_weight)).reshape(packed_length, KEY_VALUE_HEADS, 2, HEAD_SIZE)
    rotary_keys = rotate(unrotated_key_value[:, :, 0], cosine[:, None, :], sine[:, None, :])
    key_value_rows = reduced_precision(jnp.stack([rotary_keys, unrotated_key_value[:, :, 1]], axis=2).reshape(packed_length, 2 * KEY_VALUE_HEADS * HEAD_SIZE))
    attended = reduced_precision(reduced_precision_backward(attend(queries, key_value_rows, segments)))
    attn_branch = reduced_precision_backward(accurate_product(attended, w_attn_out))
    gate_z = reduced_precision_backward(accurate_product(normalized_input, w_gate_z))
    raw_x = reduced_precision(reduced_precision_backward(accurate_product(normalized_input, w_ssm_in)))
    step_raw = reduced_precision_backward(accurate_product(normalized_input, w_step))
    raw_bc = reduced_precision(reduced_precision_backward(accurate_product(normalized_input, w_bc)))
    reach = TAPS - 1
    seg_ext = jnp.concatenate([jnp.full((reach,), -1, jnp.int32), segments.astype(jnp.int32)])
    conv_x = conv_silu(jnp.concatenate([jnp.zeros((reach, DS), jnp.float32), raw_x]), w_conv_x, conv_x_bias, seg_ext)
    conv_bc = conv_silu(jnp.concatenate([jnp.zeros((reach, 2 * NS), jnp.float32), raw_bc]), w_conv_bc, conv_bc_bias, seg_ext)
    steps = jax.nn.softplus(step_raw + step_bias)
    inputs_heads = conv_x.reshape(packed_length, MH, MP)
    scanned = ssm_group(inputs_heads, conv_bc[:, :NS], conv_bc[:, NS:], steps, decay_log, segments)
    scanned = scanned + skip_gain[None, :, None] * inputs_heads
    gated = reduced_precision(reduced_precision_backward(scanned.reshape(packed_length, MH * MP) * jax.nn.silu(gate_z)))
    ssm_branch = reduced_precision_backward(accurate_product(gated, w_ssm_out))
    middle = hidden_in + attn_branch + ssm_branch
    normed_ffn = reduced_precision(middle * rms_scale(middle) * gain_ffn)
    gate_value = reduced_precision_backward(accurate_product(normed_ffn, w_gate))
    up_value = reduced_precision_backward(accurate_product(normed_ffn, w_up))
    active = reduced_precision(reduced_precision_backward(jax.nn.silu(gate_value) * up_value))
    return middle + reduced_precision_backward(accurate_product(active, w_down))

def reference(tokens, segment, gain_attn, w_query, key_value_weight, w_attn_out, w_gate_z, w_ssm_in, w_step, w_bc, w_conv_x, conv_x_bias, w_conv_bc, conv_bc_bias, step_bias, decay_log, skip_gain, w_ssm_out, gain_ffn, w_gate, w_up, w_down, grad_out):
    params = jax.tree.map(lambda weight: weight.astype(jnp.float32), (gain_attn, w_query, key_value_weight, w_attn_out, w_gate_z, w_ssm_in, w_step, w_bc, w_conv_x, conv_x_bias, w_conv_bc, conv_bc_bias, step_bias, decay_log, skip_gain, w_ssm_out, gain_ffn, w_gate, w_up, w_down))
    group_size = TOK_DEV * N_CTX
    groups = TOKENS // group_size

    def per_group(totals, operands):
        hidden_in, segments, cotangent = operands
        outputs, backward = jax.vjp(lambda weights, values: layer(weights, values, segments), params, hidden_in)
        gradients, grad_in = backward(cotangent)
        totals = jax.tree.map(lambda former, latter: former + latter, totals, gradients)
        return (totals, (outputs.astype(jnp.bfloat16), grad_in.astype(jnp.bfloat16)))
    initial = jax.tree.map(jnp.zeros_like, params)
    totals, (outputs, grad_in) = lax.scan(per_group, initial, (tokens.astype(jnp.float32).reshape(groups, group_size, MODEL_WIDTH), segment.reshape(groups, group_size), grad_out.astype(jnp.float32).reshape(groups, group_size, MODEL_WIDTH)))
    return (outputs.reshape(TOKENS, MODEL_WIDTH), grad_in.reshape(TOKENS, MODEL_WIDTH), totals[0], totals[1], totals[2], totals[3], totals[4], totals[5], totals[6], totals[7], totals[8], totals[9], totals[10], totals[11], totals[12], totals[13], totals[14], totals[15], totals[16], totals[17], totals[18], totals[19])
```

```python
from functools import partial

import jax
import jax.numpy as jnp
from jax import lax
from jax.experimental import pallas as pl
from jax.experimental.pallas import tpu as pltpu
from jax.sharding import PartitionSpec as P

HEAD_SIZE = 64
MP = 64
NS = 128
SPAN = 128
TAPS = 4
QUERY_ROWS = 64
VMEM_BYTES = 48 * 1024 * 1024


HIGHEST = lax.Precision.HIGHEST
ROPE_BASE = 100000000000.0


def rms_scale(values):
    return lax.rsqrt(jnp.mean(values * values, axis=-1, keepdims=True) + 1e-05)


def norm_back(values, scale, gain, d_normed):
    scaled = d_normed * gain[None, :]
    d_values = scale * scaled - values * scale**3 * jnp.mean(
        scaled * values, axis=-1, keepdims=True
    )
    return (d_values, jnp.sum(d_normed * values * scale, axis=0))


def contract_rows(former, latter):
    return lax.dot_general(
        former, latter, (((0,), (0,)), ((), ())), preferred_element_type=jnp.float32
    )


def contract_cols(former, latter):
    return lax.dot_general(
        former, latter, (((1,), (1,)), ((), ())), preferred_element_type=jnp.float32
    )


def silu_slope(values):
    sigma = jax.nn.sigmoid(values)
    return sigma * (1.0 + values * (1.0 - sigma))


def positions_in_group(segments):
    count = segments.shape[0]
    index = jnp.arange(count, dtype=jnp.int32)
    fresh = jnp.concatenate([jnp.ones((1,), bool), segments[1:] != segments[:-1]])
    starts = lax.cummax(jnp.where(fresh, index, 0), axis=0)
    return index - starts


def conv_silu(extended, taps, bias, seg_ext):
    reach = taps.shape[0] - 1
    packed_length = extended.shape[0] - reach
    current = seg_ext[reach:]
    total = jnp.zeros((packed_length, extended.shape[1]), jnp.float32) + bias[None, :]
    for delay in range(taps.shape[0]):
        source = extended[reach - delay : reach - delay + packed_length]
        same = (seg_ext[reach - delay : reach - delay + packed_length] == current)[:, None]
        total = total + jnp.where(same, taps[delay][None, :] * source, 0.0)
    return jax.nn.silu(total)


def dot_nn(a, b):
    return lax.dot_general(a, b, (((1,), (0,)), ((), ())), preferred_element_type=jnp.float32)


def rope_tables(positions, width):
    lane = jnp.arange(width, dtype=jnp.int32) % (HEAD_SIZE // 2)
    frequency = ROPE_BASE ** (-(2.0 * lane.astype(jnp.float32)) / HEAD_SIZE)
    angle = positions.astype(jnp.float32)[:, None] * frequency[None, :]
    return (jnp.cos(angle), jnp.sin(angle))


def rotate(values, cosine, sine):
    half = HEAD_SIZE // 2
    lane = lax.broadcasted_iota(jnp.int32, values.shape, 1) % HEAD_SIZE
    turned = jnp.where(lane < half, -jnp.roll(values, -half, 1), jnp.roll(values, half, 1))
    return values * cosine + turned * sine


def tp_sum(values):
    low = values.astype(jnp.bfloat16)
    other = lax.ppermute(low, "tp", [(0, 1), (1, 0)])
    return low.astype(jnp.float32) + other.astype(jnp.float32)


def stack_heads(block, heads):
    return jnp.concatenate(
        [block[:, h * HEAD_SIZE : (h + 1) * HEAD_SIZE] for h in range(heads)], axis=0
    )


def masked_scores(q, keys, low_ref, high_ref, heads):
    scores = contract_cols(q, keys) * (HEAD_SIZE**-0.5)
    place = lax.broadcasted_iota(jnp.int32, scores.shape, 1)
    low = jnp.concatenate([low_ref[...]] * heads, axis=0)
    high = jnp.concatenate([high_ref[...]] * heads, axis=0)
    return jnp.where((place >= low) & (place <= high), scores, -1e30)


def attn_fwd_kernel(heads, q_ref, kv_ref, low_ref, high_ref, out_ref, lse_ref):
    rows = q_ref.shape[0]
    q = stack_heads(q_ref[...], heads)
    scores = masked_scores(q, kv_ref[:, :HEAD_SIZE], low_ref, high_ref, heads)
    top = jnp.max(scores, axis=1, keepdims=True)
    expon = jnp.exp(scores - top)
    total = jnp.sum(expon, axis=1, keepdims=True)
    out = dot_nn(expon.astype(jnp.bfloat16), kv_ref[:, HEAD_SIZE:]) / total
    for h in range(heads):
        out_ref[:, h * HEAD_SIZE : (h + 1) * HEAD_SIZE] = out[h * rows : (h + 1) * rows]
    lse_ref[...] = top + jnp.log(total)


def attn_bwd_kernel(
    heads, q_ref, kv_ref, low_ref, high_ref, out_ref, lse_ref, do_ref, dq_ref, dkv_ref
):
    rows = q_ref.shape[0]
    scaling = HEAD_SIZE**-0.5

    @pl.when(pl.program_id(0) == 0)
    def _():
        dkv_ref[...] = jnp.zeros_like(dkv_ref)

    q = stack_heads(q_ref[...], heads)
    d_out = stack_heads(do_ref[...], heads)
    delta = jnp.sum(
        d_out.astype(jnp.float32) * stack_heads(out_ref[...], heads), axis=1, keepdims=True
    )
    keys = kv_ref[:, :HEAD_SIZE]
    scores = masked_scores(q, keys, low_ref, high_ref, heads)
    probs = jnp.exp(scores - lse_ref[...])
    d_probs = contract_cols(d_out, kv_ref[:, HEAD_SIZE:])
    d_scores = (probs * (d_probs - delta)).astype(jnp.bfloat16)
    dq = dot_nn(d_scores, keys) * scaling
    for h in range(heads):
        dq_ref[:, h * HEAD_SIZE : (h + 1) * HEAD_SIZE] = dq[h * rows : (h + 1) * rows]
    dkv_ref[:, :HEAD_SIZE] += contract_rows(d_scores, q) * scaling
    dkv_ref[:, HEAD_SIZE:] += contract_rows(probs.astype(jnp.bfloat16), d_out)


def attn_specs(width, keys, heads):
    rows = pl.BlockSpec((QUERY_ROWS, width), lambda i: (i, 0))
    group = pl.BlockSpec((keys, 2 * HEAD_SIZE), lambda i: (0, 0))
    column = pl.BlockSpec((QUERY_ROWS, 1), lambda i: (i, 0))
    stacked = pl.BlockSpec((QUERY_ROWS * heads, 1), lambda i: (i, 0))
    return (rows, group, column, stacked)


def attn_forward(queries, kv, low, high):
    count, width = queries.shape
    heads = width // HEAD_SIZE
    rows, group, column, stacked = attn_specs(width, kv.shape[0], heads)
    return pl.pallas_call(
        partial(attn_fwd_kernel, heads),
        grid=(count // QUERY_ROWS,),
        in_specs=[rows, group, column, column],
        out_specs=[rows, stacked],
        out_shape=[
            jax.ShapeDtypeStruct((count, width), jnp.float32),
            jax.ShapeDtypeStruct((count * heads, 1), jnp.float32),
        ],
        compiler_params=pltpu.CompilerParams(vmem_limit_bytes=VMEM_BYTES),
        cost_estimate=pl.CostEstimate(
            flops=4 * count * kv.shape[0] * width,
            bytes_accessed=4 * count * width,
            transcendentals=count * heads * kv.shape[0],
        ),
        name="attn_forward",
    )(queries, kv, low, high)


def attn_backward(queries, kv, low, high, out, lse, d_out):
    count, width = queries.shape
    heads = width // HEAD_SIZE
    rows, group, column, stacked = attn_specs(width, kv.shape[0], heads)
    return pl.pallas_call(
        partial(attn_bwd_kernel, heads),
        grid=(count // QUERY_ROWS,),
        in_specs=[rows, group, column, column, rows, stacked, rows],
        out_specs=[rows, group],
        out_shape=[
            jax.ShapeDtypeStruct((count, width), jnp.float32),
            jax.ShapeDtypeStruct(kv.shape, jnp.float32),
        ],
        compiler_params=pltpu.CompilerParams(vmem_limit_bytes=VMEM_BYTES),
        cost_estimate=pl.CostEstimate(
            flops=10 * count * kv.shape[0] * width,
            bytes_accessed=8 * count * width,
            transcendentals=count * heads * kv.shape[0],
        ),
        name="attn_backward",
    )(queries, kv, low, high, out, lse, d_out)


def pair_lanes(columns, pair, shape):
    lane = lax.broadcasted_iota(jnp.int32, shape, 1)
    return jnp.where(
        lane < MP, columns[:, 2 * pair : 2 * pair + 1], columns[:, 2 * pair + 1 : 2 * pair + 2]
    )


def split_pair(values):
    lane = lax.broadcasted_iota(jnp.int32, values.shape, 1)
    zero = jnp.zeros_like(values)
    return jnp.concatenate(
        [jnp.where(lane < MP, values, zero), jnp.where(lane < MP, zero, values)], axis=0
    )


def span_mask(segc_ref, segr_ref):
    row = lax.broadcasted_iota(jnp.int32, (SPAN, SPAN), 0)
    col = lax.broadcasted_iota(jnp.int32, (SPAN, SPAN), 1)
    return (row >= col) & (segc_ref[...] == segr_ref[...])


def head_decay(mask, cum, cum_t_ref, head):
    spread = cum[:, head : head + 1] - cum_t_ref[head : head + 1, :]
    return jnp.where(mask, jnp.exp(jnp.minimum(spread, 0.0)), 0.0)


def pair_keep(entry, pair):
    row = lax.broadcasted_iota(jnp.int32, (2 * MP, NS), 0)
    last = entry[SPAN - 1 : SPAN, :]
    return jnp.where(
        row < MP, last[:, 2 * pair : 2 * pair + 1], last[:, 2 * pair + 1 : 2 * pair + 2]
    )


def outer_kernel(pairs, v_ref, w_ref, m_ref, out_ref):
    weights = w_ref[...]
    other = m_ref[...]
    for pair in range(pairs):
        block = v_ref[:, pair * 2 * MP : (pair + 1) * 2 * MP]
        block = (block * pair_lanes(weights, pair, block.shape)).astype(jnp.bfloat16)
        out_ref[pair * 2 * MP : (pair + 1) * 2 * MP, :] = contract_rows(block, other)


def weighted_outer(values, weights, other):
    return pl.pallas_call(
        partial(outer_kernel, values.shape[1] // (2 * MP)),
        out_shape=jax.ShapeDtypeStruct((values.shape[1], other.shape[1]), jnp.float32),
        compiler_params=pltpu.CompilerParams(vmem_limit_bytes=VMEM_BYTES),
        name="weighted_outer",
    )(values, weights, other)


def ssm_fwd_kernel(
    pairs,
    x_ref, b_ref, c_ref, step_ref, cum_ref, cum_t_ref, entry_ref, ending_ref, segc_ref, segr_ref,
    init_ref, y_ref, start_ref, state_ref,
):
    @pl.when(pl.program_id(0) == 0)
    def _():
        state_ref[...] = init_ref[...]

    start_ref[0] = state_ref[...]
    b_part, c_part = b_ref[...], c_ref[...]
    steps, cum, entry, ending = step_ref[...], cum_ref[...], entry_ref[...], ending_ref[...]
    mask = span_mask(segc_ref, segr_ref)
    meet = contract_cols(c_part, b_part)
    for pair in range(pairs):
        lanes = slice(pair * 2 * MP, (pair + 1) * 2 * MP)
        shape = (SPAN, 2 * MP)
        inflow = x_ref[:, lanes] * pair_lanes(steps, pair, shape)
        weights = jnp.concatenate(
            [meet * head_decay(mask, cum, cum_t_ref, 2 * pair + k) for k in range(2)], axis=1
        ).astype(jnp.bfloat16)
        state = state_ref[lanes, :]
        y_ref[:, lanes] = dot_nn(weights, split_pair(inflow.astype(jnp.bfloat16))) + pair_lanes(
            entry, pair, shape
        ) * contract_cols(c_part, state.astype(jnp.bfloat16))
        late = (inflow * pair_lanes(ending, pair, shape)).astype(jnp.bfloat16)
        state_ref[lanes, :] = pair_keep(entry, pair) * state + contract_rows(late, b_part)


def ssm_bwd_kernel(
    pairs,
    x_ref, b_ref, c_ref, step_ref, cum_ref, cum_t_ref, entry_ref, ending_ref, segc_ref, segr_ref,
    init_ref, y_ref, start_ref, dy_ref, skip_ref,
    dx_ref, db_ref, dc_ref, dcum_ref, dstep_ref, state_ref,
):
    @pl.when(pl.program_id(0) == 0)
    def _():
        state_ref[...] = init_ref[...]

    b_part, c_part = b_ref[...], c_ref[...]
    steps, cum, entry, ending = step_ref[...], cum_ref[...], entry_ref[...], ending_ref[...]
    mask = span_mask(segc_ref, segr_ref)
    meet = contract_cols(c_part, b_part)
    d_meet = jnp.zeros((SPAN, SPAN), jnp.float32)
    d_b = jnp.zeros((SPAN, NS), jnp.float32)
    d_c = jnp.zeros((SPAN, NS), jnp.float32)
    lane = lax.broadcasted_iota(jnp.int32, (SPAN, 2 * MP), 1)
    token = lax.broadcasted_iota(jnp.int32, (SPAN, 1), 0)
    for pair in range(pairs):
        lanes = slice(pair * 2 * MP, (pair + 1) * 2 * MP)
        shape = (SPAN, 2 * MP)
        x = x_ref[:, lanes]
        step_lanes = pair_lanes(steps, pair, shape)
        end_lanes = pair_lanes(ending, pair, shape)
        inflow = x * step_lanes
        inflow_low = inflow.astype(jnp.bfloat16)
        dy = dy_ref[:, lanes]
        dy_low = dy.astype(jnp.bfloat16)
        dy_split = split_pair(dy_low)
        decays = jnp.concatenate(
            [head_decay(mask, cum, cum_t_ref, 2 * pair + k) for k in range(2)], axis=0
        )
        weights = (jnp.concatenate([meet, meet], axis=0) * decays).astype(jnp.bfloat16)
        grown = contract_cols(dy_split, inflow_low) * decays
        d_meet = d_meet + grown[:SPAN] + grown[SPAN:]
        d_state = state_ref[lanes, :]
        d_state_low = d_state.astype(jnp.bfloat16)
        start = start_ref[0, lanes, :]
        from_end = end_lanes * contract_cols(b_part, d_state_low)
        d_inflow = contract_rows(weights, dy_split) + from_end
        late = (inflow * end_lanes).astype(jnp.bfloat16)
        d_b = d_b + dot_nn(late, d_state_low)
        early = (dy * pair_lanes(entry, pair, shape)).astype(jnp.bfloat16)
        d_c = d_c + dot_nn(early, start.astype(jnp.bfloat16))
        keep = pair_keep(entry, pair)
        kept = keep * d_state * start
        state_ref[lanes, :] = keep * d_state + contract_rows(early, c_part)
        inflow_wide = inflow_low.astype(jnp.float32)
        balance = dy_low.astype(jnp.float32) * y_ref[:, lanes] - inflow_wide * d_inflow
        ended = inflow_wide * from_end
        direct = x * d_inflow
        for k in range(2):
            own = (lane < MP) if k == 0 else (lane >= MP)
            head = 2 * pair + k
            total = jnp.sum(
                jnp.sum(jnp.where(own, ended, 0.0), axis=1, keepdims=True), axis=0, keepdims=True
            ) + jnp.sum(
                jnp.sum(kept[k * MP : (k + 1) * MP], axis=1, keepdims=True), axis=0, keepdims=True
            )
            column = jnp.sum(jnp.where(own, balance, 0.0), axis=1, keepdims=True)
            dcum_ref[:, head : head + 1] = column + jnp.where(token == SPAN - 1, total, 0.0)
            dstep_ref[:, head : head + 1] = jnp.sum(
                jnp.where(own, direct, 0.0), axis=1, keepdims=True
            )
        dx_ref[:, lanes] = step_lanes * d_inflow + skip_ref[:, lanes] * dy
    d_meet_low = d_meet.astype(jnp.bfloat16)
    dc_ref[...] = d_c + dot_nn(d_meet_low, b_part)
    db_ref[...] = d_b + contract_rows(d_meet_low, c_part)


def ssm_specs(count, inner, heads, backward):
    spans = count // SPAN

    def at(i):
        return spans - 1 - i if backward else i

    wide = pl.BlockSpec((SPAN, inner), lambda i: (at(i), 0))
    narrow = pl.BlockSpec((SPAN, NS), lambda i: (at(i), 0))
    per_head = pl.BlockSpec((SPAN, heads), lambda i: (at(i), 0))
    turned = pl.BlockSpec((heads, SPAN), lambda i: (0, at(i)))
    seg_col = pl.BlockSpec((SPAN, 1), lambda i: (at(i), 0))
    seg_row = pl.BlockSpec((1, SPAN), lambda i: (0, at(i)))
    whole = pl.BlockSpec((inner, NS), lambda i: (0, 0))
    starts = pl.BlockSpec((1, inner, NS), lambda i: (at(i), 0, 0))
    flat = pl.BlockSpec((1, inner), lambda i: (0, 0))
    inputs = [wide, narrow, narrow, per_head, per_head, turned, per_head, per_head]
    inputs += [seg_col, seg_row, whole]
    return inputs, wide, narrow, per_head, starts, flat


def ssm_forward(operands, state_in):
    count, inner = operands[0].shape
    heads = operands[3].shape[1]
    inputs, wide, narrow, per_head, starts, flat = ssm_specs(count, inner, heads, False)
    return pl.pallas_call(
        partial(ssm_fwd_kernel, heads // 2),
        grid=(count // SPAN,),
        in_specs=inputs,
        out_specs=[wide, starts],
        out_shape=[
            jax.ShapeDtypeStruct((count, inner), jnp.float32),
            jax.ShapeDtypeStruct((count // SPAN, inner, NS), jnp.float32),
        ],
        scratch_shapes=[pltpu.VMEM((inner, NS), jnp.float32)],
        compiler_params=pltpu.CompilerParams(vmem_limit_bytes=VMEM_BYTES),
        name="ssm_forward",
    )(*operands, state_in)


def ssm_backward(operands, state_grad, y, starting, dy, skip):
    count, inner = operands[0].shape
    heads = operands[3].shape[1]
    inputs, wide, narrow, per_head, starts, flat = ssm_specs(count, inner, heads, True)
    return pl.pallas_call(
        partial(ssm_bwd_kernel, heads // 2),
        grid=(count // SPAN,),
        in_specs=inputs + [wide, starts, wide, flat],
        out_specs=[wide, narrow, narrow, per_head, per_head],
        out_shape=[
            jax.ShapeDtypeStruct((count, inner), jnp.float32),
            jax.ShapeDtypeStruct((count, NS), jnp.float32),
            jax.ShapeDtypeStruct((count, NS), jnp.float32),
            jax.ShapeDtypeStruct((count, heads), jnp.float32),
            jax.ShapeDtypeStruct((count, heads), jnp.float32),
        ],
        scratch_shapes=[pltpu.VMEM((inner, NS), jnp.float32)],
        compiler_params=pltpu.CompilerParams(vmem_limit_bytes=VMEM_BYTES),
        name="ssm_backward",
    )(*operands, state_grad, y, starting, dy, skip)


def span_cumulative(values):
    count, heads = values.shape
    index = jnp.arange(SPAN)
    lower = (index[:, None] >= index[None, :]).astype(jnp.float32)
    spans = values.reshape(count // SPAN, SPAN, heads)
    return jnp.einsum("tu,cuh->cth", lower, spans, precision=HIGHEST).reshape(count, heads)


def span_reverse_cumulative(values):
    count, heads = values.shape
    index = jnp.arange(SPAN)
    upper = (index[:, None] <= index[None, :]).astype(jnp.float32)
    spans = values.reshape(count // SPAN, SPAN, heads)
    return jnp.einsum("tu,cuh->cth", upper, spans, precision=HIGHEST).reshape(count, heads)


def decay_tables(steps, decay_log, seg_local, seg_before):
    count, heads = steps.shape
    spans = count // SPAN
    cum = span_cumulative(steps * (-jnp.exp(decay_log))[None, :])
    by_span = cum.reshape(spans, SPAN, heads)
    seg_spans = seg_local.reshape(spans, SPAN)
    seg_last = seg_spans[:, -1]
    seg_prev = jnp.concatenate([seg_before[None], seg_last[:-1]])
    totals = by_span[:, -1]
    entry = jnp.where((seg_spans == seg_prev[:, None])[..., None], jnp.exp(by_span), 0.0)
    ending = jnp.where(
        (seg_spans == seg_last[:, None])[..., None], jnp.exp(totals[:, None] - by_span), 0.0
    )
    sums = [jnp.zeros_like(totals[0])]
    for span in range(spans):
        sums.append(sums[-1] + totals[span])
    whole = (jnp.stack(sums[:-1])[:, None] + by_span).reshape(count, heads)
    grand = sums[-1]
    seg_end = seg_local[-1]
    entry_all = jnp.where((seg_local == seg_before)[:, None], jnp.exp(whole), 0.0)
    ending_all = jnp.where((seg_local == seg_end)[:, None], jnp.exp(grand[None] - whole), 0.0)
    through = jnp.where(seg_end == seg_before, jnp.exp(grand), 0.0)
    return (
        cum,
        entry.reshape(count, heads),
        ending.reshape(count, heads),
        entry_all,
        ending_all,
        through,
    )


def join_states(states, through, forward):
    length, place = (lax.axis_size("ctx"), lax.axis_index("ctx"))
    order = range(length - 1, -1, -1) if forward else range(length)
    factor = jnp.ones_like(through[0])
    total = jnp.zeros(states.shape[1:], jnp.float32)
    for k in order:
        reached = (k < place) if forward else (k > place)
        weight = jnp.repeat(jnp.where(reached, factor, 0.0), MP)
        total = total + weight[:, None] * states[k].astype(jnp.float32)
        factor = jnp.where(reached, factor * through[k], factor)
    return total


def local(
    tokens, segment, gain_attn, w_query, key_value_weight, w_attn_out, w_gate_z, w_ssm_in, w_step,
    w_bc, w_conv_x, conv_x_bias, w_conv_bc, conv_bc_bias, step_bias, decay_log, skip_gain,
    w_ssm_out, gain_ffn, w_gate, w_up, w_down, grad_out,
):
    qn, kn = w_query.shape[1], key_value_weight.shape[1]
    zn, xn, bn, sn = w_gate_z.shape[1], w_ssm_in.shape[1], w_bc.shape[1], w_step.shape[1]
    fn = w_gate.shape[1]
    an = w_attn_out.shape[0]
    q0, k0, z0, x0 = 0, qn, qn + kn, qn + kn + zn
    b0 = x0 + xn
    s0 = b0 + bn
    g0 = s0 + sn
    first_pack = jnp.concatenate(
        [w_query, key_value_weight, w_gate_z, w_ssm_in, w_bc, w_step]
        + [gain_attn[:, None], gain_ffn[:, None]],
        axis=1,
    )
    out_pack = jnp.concatenate([w_attn_out, w_ssm_out], axis=0).T
    ffn_pack = jnp.concatenate([w_gate, w_up], axis=1)
    full_first = lax.all_gather(first_pack, "shard", axis=0, tiled=True)
    full_out = lax.all_gather(out_pack, "shard", axis=0, tiled=True)
    full_ffn = lax.all_gather(ffn_pack, "shard", axis=0, tiled=True)
    full_down = lax.all_gather(w_down.T, "shard", axis=0, tiled=True)

    row_count = tokens.shape[0]
    ctx_rank = lax.axis_index("ctx")
    ctx_count = lax.axis_size("ctx")
    first_row = ctx_rank * row_count
    seg_local = lax.dynamic_slice_in_dim(segment, first_row, row_count)
    seg_before = jnp.where(
        ctx_rank > 0, lax.dynamic_slice_in_dim(segment, jnp.maximum(first_row - 1, 0), 1)[0], -1
    )
    reach = TAPS - 1
    positions = lax.dynamic_slice_in_dim(positions_in_group(segment), first_row, row_count)
    cos_q, sin_q = rope_tables(positions, qn)
    cosine, sine = cos_q[:, :HEAD_SIZE], sin_q[:, :HEAD_SIZE]
    high = (first_row + jnp.arange(row_count, dtype=jnp.int32))[:, None]
    low = high - positions[:, None]
    seg_padded = jnp.concatenate([jnp.full((reach,), -1, jnp.int32), segment])
    seg_ext = lax.dynamic_slice_in_dim(seg_padded, first_row, row_count + reach)
    hidden_in = tokens.astype(jnp.float32)
    gains = full_first[:, g0:].astype(jnp.float32).T
    gain_one, gain_two = gains[0], gains[1]
    scale_one = rms_scale(hidden_in)
    normalized_input = (hidden_in * scale_one * gain_one[None, :]).astype(jnp.bfloat16)
    proj = jnp.dot(normalized_input, full_first, preferred_element_type=jnp.float32)
    queries = rotate(proj[:, q0:k0], cos_q, sin_q).astype(jnp.bfloat16)
    keyval_raw = proj[:, k0:z0]
    keyval = jnp.concatenate(
        [rotate(keyval_raw[:, :HEAD_SIZE], cosine, sine), keyval_raw[:, HEAD_SIZE:]], axis=-1
    ).astype(jnp.bfloat16)
    raw_x = proj[:, x0:b0].astype(jnp.bfloat16)
    raw_bc = proj[:, b0:s0].astype(jnp.bfloat16)
    gate_z = proj[:, z0:x0]
    step_raw = proj[:, s0:g0]
    onward = [(k, k + 1) for k in range(ctx_count - 1)]
    backward = [(k + 1, k) for k in range(ctx_count - 1)]
    tails = lax.ppermute(
        jnp.concatenate([raw_x[row_count - reach :], raw_bc[row_count - reach :]], axis=1),
        "ctx",
        onward,
    )
    all_keys = lax.all_gather(keyval, "ctx", axis=0, tiled=True)

    ext_x = jnp.concatenate([tails[:, :xn], raw_x], axis=0).astype(jnp.float32)
    ext_bc = jnp.concatenate([tails[:, xn:], raw_bc], axis=0).astype(jnp.float32)
    conv_x, conv_x_back = jax.vjp(
        lambda extended, taps, bias: conv_silu(extended, taps, bias, seg_ext),
        ext_x,
        w_conv_x,
        conv_x_bias,
    )
    conv_bc, conv_bc_back = jax.vjp(
        lambda extended, taps, bias: conv_silu(extended, taps, bias, seg_ext),
        ext_bc,
        w_conv_bc,
        conv_bc_bias,
    )
    steps = jax.nn.softplus(step_raw + step_bias[None, :])
    mamba_local = step_bias.shape[0]
    b_low = conv_bc[:, :NS].astype(jnp.bfloat16)
    c_low = conv_bc[:, NS:].astype(jnp.bfloat16)
    cum, entry, ending, entry_all, ending_all, through = decay_tables(
        steps, decay_log, seg_local, seg_before
    )
    local_state = weighted_outer(conv_x, steps * ending_all, b_low)
    through_row = jnp.zeros((16, NS), jnp.float32).at[0, :mamba_local].set(through)
    state_parts = lax.all_gather(
        jnp.concatenate([local_state, through_row], axis=0).astype(jnp.bfloat16), "ctx"
    )
    attn_out, lse = attn_forward(queries, all_keys, low, high)
    attended = attn_out.astype(jnp.bfloat16)
    all_through = state_parts[:, xn, :mamba_local].astype(jnp.float32)
    state_in = join_states(state_parts[:, :xn], all_through, True)
    operands = (
        conv_x, b_low, c_low, steps, cum, cum.T, entry, ending, seg_local[:, None],
        seg_local[None, :],
    )
    skip_row = jnp.repeat(skip_gain, MP)[None, :]
    y_scan, starting = ssm_forward(operands, state_in)
    scanned = y_scan + skip_row * conv_x
    silu_gate = jax.nn.silu(gate_z)
    gated = (scanned * silu_gate).astype(jnp.bfloat16)
    mixer = jnp.concatenate([attended, gated], axis=1)
    middle = hidden_in + tp_sum(contract_cols(mixer, full_out))

    scale_two = rms_scale(middle)
    normed_ffn = (middle * scale_two * gain_two[None, :]).astype(jnp.bfloat16)
    gate_up = jnp.dot(normed_ffn, full_ffn, preferred_element_type=jnp.float32)
    gate_value, up_value = gate_up[:, :fn], gate_up[:, fn:]
    active = (jax.nn.silu(gate_value) * up_value).astype(jnp.bfloat16)
    d_active = (
        jnp.dot(grad_out, full_down, preferred_element_type=jnp.float32)
        .astype(jnp.bfloat16)
        .astype(jnp.float32)
    )
    d_gate_up = jnp.concatenate(
        [
            (d_active * up_value * silu_slope(gate_value)).astype(jnp.bfloat16),
            (d_active * jax.nn.silu(gate_value)).astype(jnp.bfloat16),
        ],
        axis=1,
    )
    d_normed_ffn = tp_sum(contract_cols(d_gate_up, full_ffn))
    down_part = contract_cols(active, full_down)
    result = (middle + tp_sum(down_part)).astype(jnp.bfloat16)
    grad_down_t = contract_rows(grad_out, active)
    grad_ffn = contract_rows(normed_ffn, d_gate_up)

    def scatter(values):
        part = lax.psum_scatter(
            values.astype(jnp.bfloat16), "shard", scatter_dimension=0, tiled=True
        )
        return lax.psum(part, "ctx").astype(jnp.float32)

    sum_ffn = scatter(jnp.concatenate([grad_ffn, grad_down_t], axis=1))

    d_from_ffn, grad_gain_two = norm_back(middle, scale_two, gain_two, d_normed_ffn)
    d_middle = grad_out.astype(jnp.float32) + d_from_ffn
    d_mid_low = d_middle.astype(jnp.bfloat16)
    d_mixer = jnp.dot(d_mid_low, full_out, preferred_element_type=jnp.float32).astype(jnp.bfloat16)
    d_attended = d_mixer[:, :an]
    d_gated = d_mixer[:, an:].astype(jnp.float32)
    d_scanned = d_gated * silu_gate
    d_gate_z = (d_gated * scanned * silu_slope(gate_z)).astype(jnp.bfloat16)
    grad_skip = jnp.sum((d_scanned * conv_x).reshape(row_count, mamba_local, MP), axis=(0, 2))
    d_state_local = weighted_outer(d_scanned, entry_all, c_low)
    d_state_parts = lax.all_gather(d_state_local.astype(jnp.bfloat16), "ctx")
    d_query, d_kv_group = attn_backward(queries, all_keys, low, high, attn_out, lse, d_attended)
    d_kv_back = lax.psum_scatter(
        d_kv_group.astype(jnp.bfloat16), "ctx", scatter_dimension=0, tiled=True
    ).astype(jnp.float32)
    sum_out = scatter(contract_rows(d_mid_low, mixer))
    state_grad = join_states(d_state_parts, all_through, False)
    d_x_post, d_b, d_c, d_cum, d_direct = ssm_backward(
        operands, state_grad, y_scan, starting, d_scanned, skip_row
    )
    d_log = span_reverse_cumulative(d_cum)
    rates = -jnp.exp(decay_log)[None, :]
    grad_decay = jnp.sum(d_log * steps * rates, axis=0)
    d_steps = d_log * rates + d_direct
    d_bc_post = jnp.concatenate([d_b, d_c], axis=-1)
    d_ext_x, grad_convx_taps, grad_convx_bias = conv_x_back(d_x_post)
    d_ext_bc, grad_convbc_taps, grad_convbc_bias = conv_bc_back(d_bc_post)
    d_pre = d_steps * jax.nn.sigmoid(step_raw + step_bias[None, :])
    grad_bias = jnp.sum(d_pre, axis=0)
    back_tails = lax.ppermute(
        jnp.concatenate([d_ext_x[:reach], d_ext_bc[:reach]], axis=1).astype(jnp.bfloat16),
        "ctx",
        backward,
    ).astype(jnp.float32)
    d_keyval = jnp.concatenate(
        [rotate(d_kv_back[:, :HEAD_SIZE], cosine, -sine), d_kv_back[:, HEAD_SIZE:]], axis=-1
    ).astype(jnp.bfloat16)
    d_queries = rotate(d_query, cos_q, -sin_q).astype(jnp.bfloat16)
    last = row_count - reach
    d_raw_x = d_ext_x[reach:].at[last:].add(back_tails[:, :xn]).astype(jnp.bfloat16)
    d_bc_part = d_ext_bc[reach:].at[last:].add(back_tails[:, xn:]).astype(jnp.bfloat16)
    d_bc_other = lax.ppermute(d_bc_part, "tp", [(0, 1), (1, 0)])
    d_bc = (d_bc_part.astype(jnp.float32) + d_bc_other.astype(jnp.float32)).astype(jnp.bfloat16)
    d_proj = jnp.concatenate(
        [d_queries, d_keyval, d_gate_z, d_raw_x, d_bc_part, d_pre.astype(jnp.bfloat16)]
        + [jnp.zeros((row_count, 2), jnp.bfloat16)],
        axis=1,
    )
    d_normed = tp_sum(contract_cols(d_proj, full_first))
    d_proj_sum = jnp.concatenate(
        [d_queries, d_keyval, d_gate_z, d_raw_x, d_bc, d_pre.astype(jnp.bfloat16)], axis=1
    )
    sum_first = scatter(contract_rows(normalized_input, d_proj_sum))
    d_from_attn, grad_gain_one = norm_back(hidden_in, scale_one, gain_one, d_normed)
    grad_tokens = (d_middle + d_from_attn).astype(jnp.bfloat16)

    tp_rank = lax.axis_index("tp")
    tp_count = lax.axis_size("tp")
    per_device = jnp.concatenate(
        [grad_convx_taps, grad_convx_bias[None]], axis=0
    ).reshape(-1)
    scalars = jnp.concatenate([grad_bias, grad_decay, grad_skip])
    own = jnp.concatenate([per_device, jnp.pad(scalars, (0, 128 - scalars.shape[0]))])
    wide = lax.dynamic_update_slice_in_dim(
        jnp.zeros((tp_count * own.shape[0],), jnp.float32), own, tp_rank * own.shape[0], 0
    )
    shared = jnp.concatenate(
        [
            grad_convbc_taps.reshape(-1),
            grad_convbc_bias,
            grad_gain_one / tp_count,
            grad_gain_two / tp_count,
        ]
    )
    sums = lax.psum(jnp.concatenate([wide, shared]), ("shard", "ctx", "tp"))
    mine = lax.dynamic_slice_in_dim(sums, tp_rank * own.shape[0], own.shape[0])
    taps_sum = mine[: (TAPS + 1) * xn].reshape(TAPS + 1, xn)
    heads_sum = mine[(TAPS + 1) * xn :]
    rest = sums[tp_count * own.shape[0] :]
    convbc_sum = rest[: (TAPS + 1) * bn].reshape(TAPS + 1, bn)
    gain_sums = rest[(TAPS + 1) * bn :].reshape(2, -1)
    gain_rows = gain_attn.shape[0]
    gain_sums = lax.dynamic_slice_in_dim(
        gain_sums, lax.axis_index("shard") * gain_rows, gain_rows, 1
    )
    out_t = sum_out.T
    return (
        result,
        grad_tokens,
        gain_sums[0],
        sum_first[:, q0:k0],
        sum_first[:, k0:z0],
        out_t[:an],
        sum_first[:, z0:x0],
        sum_first[:, x0:b0],
        sum_first[:, s0:g0],
        sum_first[:, b0:s0],
        taps_sum[:TAPS],
        taps_sum[TAPS],
        convbc_sum[:TAPS],
        convbc_sum[TAPS],
        heads_sum[:mamba_local],
        heads_sum[mamba_local : 2 * mamba_local],
        heads_sum[2 * mamba_local : 3 * mamba_local],
        out_t[an:],
        gain_sums[1],
        sum_ffn[:, :fn],
        sum_ffn[:, fn : 2 * fn],
        sum_ffn[:, 2 * fn :].T,
    )


def solution(mesh):
    return jax.shard_map(
        local,
        mesh=mesh,
        in_specs=(
            P(("shard", "ctx"), None),
            P("shard"),
            P("shard"),
            P("shard", "tp"),
            P("shard", "tp"),
            P("tp", "shard"),
            P("shard", "tp"),
            P("shard", "tp"),
            P("shard", "tp"),
            P("shard", None),
            P(None, "tp"),
            P("tp"),
            P(),
            P(),
            P("tp"),
            P("tp"),
            P("tp"),
            P("tp", "shard"),
            P("shard"),
            P("shard", "tp"),
            P("shard", "tp"),
            P("tp", "shard"),
            P(("shard", "ctx"), None),
        ),
        out_specs=(
            P(("shard", "ctx"), None),
            P(("shard", "ctx"), None),
            P("shard"),
            P("shard", "tp"),
            P("shard", "tp"),
            P("tp", "shard"),
            P("shard", "tp"),
            P("shard", "tp"),
            P("shard", "tp"),
            P("shard", None),
            P(None, "tp"),
            P("tp"),
            P(),
            P(),
            P("tp"),
            P("tp"),
            P("tp"),
            P("tp", "shard"),
            P("shard"),
            P("shard", "tp"),
            P("shard", "tp"),
            P("tp", "shard"),
        ),
        check_vma=False,
    )
```

```python
from functools import partial

import jax
import jax.numpy as jnp
from jax import lax
from jax.experimental import pallas as pl
from jax.experimental.pallas import tpu as pltpu
from jax.sharding import PartitionSpec as P

HEAD_SIZE = 64
MP = 64
NS = 128
SPAN = 128
TAPS = 4
QUERY_ROWS = 64
VMEM_BYTES = 48 * 1024 * 1024


HIGHEST = lax.Precision.HIGHEST
ROPE_BASE = 100000000000.0


def rms_scale(values):
    return lax.rsqrt(jnp.mean(values * values, axis=-1, keepdims=True) + 1e-05)


def norm_back(values, scale, gain, d_normed):
    scaled = d_normed * gain[None, :]
    d_values = scale * scaled - values * scale**3 * jnp.mean(
        scaled * values, axis=-1, keepdims=True
    )
    return (d_values, jnp.sum(d_normed * values * scale, axis=0))


def contract_rows(former, latter):
    return lax.dot_general(
        former, latter, (((0,), (0,)), ((), ())), preferred_element_type=jnp.float32
    )


def contract_cols(former, latter):
    return lax.dot_general(
        former, latter, (((1,), (1,)), ((), ())), preferred_element_type=jnp.float32
    )


def silu_slope(values):
    sigma = jax.nn.sigmoid(values)
    return sigma * (1.0 + values * (1.0 - sigma))


def positions_in_group(segments):
    count = segments.shape[0]
    index = jnp.arange(count, dtype=jnp.int32)
    fresh = jnp.concatenate([jnp.ones((1,), bool), segments[1:] != segments[:-1]])
    starts = lax.cummax(jnp.where(fresh, index, 0), axis=0)
    return index - starts


def conv_silu(extended, taps, bias, seg_ext):
    reach = taps.shape[0] - 1
    packed_length = extended.shape[0] - reach
    current = seg_ext[reach:]
    total = jnp.zeros((packed_length, extended.shape[1]), jnp.float32) + bias[None, :]
    for delay in range(taps.shape[0]):
        source = extended[reach - delay : reach - delay + packed_length]
        same = (seg_ext[reach - delay : reach - delay + packed_length] == current)[:, None]
        total = total + jnp.where(same, taps[delay][None, :] * source, 0.0)
    return jax.nn.silu(total)


def dot_nn(a, b):
    return lax.dot_general(a, b, (((1,), (0,)), ((), ())), preferred_element_type=jnp.float32)


def rope_tables(positions, width):
    lane = jnp.arange(width, dtype=jnp.int32) % (HEAD_SIZE // 2)
    frequency = ROPE_BASE ** (-(2.0 * lane.astype(jnp.float32)) / HEAD_SIZE)
    angle = positions.astype(jnp.float32)[:, None] * frequency[None, :]
    return (jnp.cos(angle), jnp.sin(angle))


def rotate(values, cosine, sine):
    half = HEAD_SIZE // 2
    lane = lax.broadcasted_iota(jnp.int32, values.shape, 1) % HEAD_SIZE
    turned = jnp.where(lane < half, -jnp.roll(values, -half, 1), jnp.roll(values, half, 1))
    return values * cosine + turned * sine


def tp_sum(values):
    low = values.astype(jnp.bfloat16)
    other = lax.ppermute(low, "tp", [(0, 1), (1, 0)])
    return low.astype(jnp.float32) + other.astype(jnp.float32)


def partners(axis, bit):
    return [(k, k ^ bit) for k in range(lax.axis_size(axis))]


def bits_of(axis):
    bit, bits = lax.axis_size(axis) // 2, []
    while bit:
        bits.append(bit)
        bit //= 2
    return bits


def gather_rows(block, axis):
    count, me = (lax.axis_size(axis), lax.axis_index(axis))
    rows = block.shape[0]
    half = rows // 2
    full = jnp.zeros((count * rows, block.shape[1]), block.dtype)
    for part, bits in enumerate((bits_of(axis), bits_of(axis)[::-1])):
        pieces = {0: block[part * half : (part + 1) * half]}
        for bit in bits:
            for offset in list(pieces):
                pieces[offset ^ bit] = lax.ppermute(pieces[offset], axis, partners(axis, bit))
        for offset, piece in pieces.items():
            place = (me ^ offset) * rows + part * half
            full = lax.dynamic_update_slice_in_dim(full, piece, place, 0)
    return full


def reduce_rows(values, axis):
    count, me = (lax.axis_size(axis), lax.axis_index(axis))
    half = values.shape[0] // count // 2
    bits = bits_of(axis)
    parts = []
    for part, order in enumerate((bits, bits[::-1])):
        total = values.reshape((2,) * len(bits) + (2, half, values.shape[1]))
        total = lax.index_in_dim(total, part, len(bits), False)
        left = list(bits)
        for bit in order:
            dim = left.index(bit)
            left.remove(bit)
            own = (me // bit) % 2
            sent = lax.dynamic_index_in_dim(total, 1 - own, dim, False).astype(jnp.bfloat16)
            kept = lax.dynamic_index_in_dim(total, own, dim, False).astype(jnp.float32)
            got = lax.ppermute(sent, axis, partners(axis, bit)).astype(jnp.float32)
            total = (kept + got).astype(jnp.bfloat16)
        parts.append(total)
    return jnp.concatenate(parts, axis=0)


def sum_over(values, axes):
    for axis in axes:
        for bit in bits_of(axis):
            values = values + lax.ppermute(values, axis, partners(axis, bit))
    return values


def shifted(values, step):
    count = lax.axis_size("ctx")
    pairs = [(k, k + step) for k in range(count) if 0 <= k + step < count]
    return lax.ppermute(values, "ctx", pairs)


def place_from(step):
    count = lax.axis_size("ctx")
    return lax.rem(lax.axis_index("ctx") - step + count, count)


def stack_heads(block, heads):
    return jnp.concatenate(
        [block[:, h * HEAD_SIZE : (h + 1) * HEAD_SIZE] for h in range(heads)], axis=0
    )


def masked_scores(q, keys, low_ref, high_ref, heads):
    scores = contract_cols(q, keys) * (HEAD_SIZE**-0.5)
    place = lax.broadcasted_iota(jnp.int32, scores.shape, 1)
    low = jnp.concatenate([low_ref[...]] * heads, axis=0)
    high = jnp.concatenate([high_ref[...]] * heads, axis=0)
    return jnp.where((place >= low) & (place <= high), scores, -1e30)


def attn_fwd_kernel(heads, q_ref, kv_ref, low_ref, high_ref, out_ref, lse_ref):
    rows = q_ref.shape[0]
    q = stack_heads(q_ref[...], heads)
    scores = masked_scores(q, kv_ref[:, :HEAD_SIZE], low_ref, high_ref, heads)
    top = jnp.max(scores, axis=1, keepdims=True)
    expon = jnp.exp(scores - top)
    total = jnp.sum(expon, axis=1, keepdims=True)
    out = dot_nn(expon.astype(jnp.bfloat16), kv_ref[:, HEAD_SIZE:]) / total
    for h in range(heads):
        out_ref[:, h * HEAD_SIZE : (h + 1) * HEAD_SIZE] = out[h * rows : (h + 1) * rows]
    lse_ref[...] = top + jnp.log(total)


def attn_bwd_kernel(
    heads, q_ref, kv_ref, low_ref, high_ref, out_ref, lse_ref, do_ref, dq_ref, dkv_ref
):
    rows = q_ref.shape[0]
    scaling = HEAD_SIZE**-0.5

    @pl.when(pl.program_id(0) == 0)
    def _():
        dkv_ref[...] = jnp.zeros_like(dkv_ref)

    q = stack_heads(q_ref[...], heads)
    d_out = stack_heads(do_ref[...], heads)
    delta = jnp.sum(
        d_out.astype(jnp.float32) * stack_heads(out_ref[...], heads), axis=1, keepdims=True
    )
    keys = kv_ref[:, :HEAD_SIZE]
    scores = masked_scores(q, keys, low_ref, high_ref, heads)
    probs = jnp.exp(scores - lse_ref[...])
    d_probs = contract_cols(d_out, kv_ref[:, HEAD_SIZE:])
    d_scores = (probs * (d_probs - delta)).astype(jnp.bfloat16)
    dq = dot_nn(d_scores, keys) * scaling
    for h in range(heads):
        dq_ref[:, h * HEAD_SIZE : (h + 1) * HEAD_SIZE] = dq[h * rows : (h + 1) * rows]
    dkv_ref[:, :HEAD_SIZE] += contract_rows(d_scores, q) * scaling
    dkv_ref[:, HEAD_SIZE:] += contract_rows(probs.astype(jnp.bfloat16), d_out)


def attn_specs(width, keys, heads):
    rows = pl.BlockSpec((QUERY_ROWS, width), lambda i: (i, 0))
    group = pl.BlockSpec((keys, 2 * HEAD_SIZE), lambda i: (0, 0))
    column = pl.BlockSpec((QUERY_ROWS, 1), lambda i: (i, 0))
    stacked = pl.BlockSpec((QUERY_ROWS * heads, 1), lambda i: (i, 0))
    return (rows, group, column, stacked)


def attn_forward(queries, kv, low, high):
    count, width = queries.shape
    heads = width // HEAD_SIZE
    rows, group, column, stacked = attn_specs(width, kv.shape[0], heads)
    return pl.pallas_call(
        partial(attn_fwd_kernel, heads),
        grid=(count // QUERY_ROWS,),
        in_specs=[rows, group, column, column],
        out_specs=[rows, stacked],
        out_shape=[
            jax.ShapeDtypeStruct((count, width), jnp.float32),
            jax.ShapeDtypeStruct((count * heads, 1), jnp.float32),
        ],
        compiler_params=pltpu.CompilerParams(vmem_limit_bytes=VMEM_BYTES),
        cost_estimate=pl.CostEstimate(
            flops=4 * count * kv.shape[0] * width,
            bytes_accessed=4 * count * width,
            transcendentals=count * heads * kv.shape[0],
        ),
        name="attn_forward",
    )(queries, kv, low, high)


def attn_backward(queries, kv, low, high, out, lse, d_out):
    count, width = queries.shape
    heads = width // HEAD_SIZE
    rows, group, column, stacked = attn_specs(width, kv.shape[0], heads)
    return pl.pallas_call(
        partial(attn_bwd_kernel, heads),
        grid=(count // QUERY_ROWS,),
        in_specs=[rows, group, column, column, rows, stacked, rows],
        out_specs=[rows, group],
        out_shape=[
            jax.ShapeDtypeStruct((count, width), jnp.float32),
            jax.ShapeDtypeStruct(kv.shape, jnp.float32),
        ],
        compiler_params=pltpu.CompilerParams(vmem_limit_bytes=VMEM_BYTES),
        cost_estimate=pl.CostEstimate(
            flops=10 * count * kv.shape[0] * width,
            bytes_accessed=8 * count * width,
            transcendentals=count * heads * kv.shape[0],
        ),
        name="attn_backward",
    )(queries, kv, low, high, out, lse, d_out)


def pair_lanes(columns, pair, shape):
    lane = lax.broadcasted_iota(jnp.int32, shape, 1)
    return jnp.where(
        lane < MP, columns[:, 2 * pair : 2 * pair + 1], columns[:, 2 * pair + 1 : 2 * pair + 2]
    )


def split_pair(values):
    lane = lax.broadcasted_iota(jnp.int32, values.shape, 1)
    zero = jnp.zeros_like(values)
    return jnp.concatenate(
        [jnp.where(lane < MP, values, zero), jnp.where(lane < MP, zero, values)], axis=0
    )


def span_mask(segc_ref, segr_ref):
    row = lax.broadcasted_iota(jnp.int32, (SPAN, SPAN), 0)
    col = lax.broadcasted_iota(jnp.int32, (SPAN, SPAN), 1)
    return (row >= col) & (segc_ref[...] == segr_ref[...])


def head_decay(mask, cum, cum_t_ref, head):
    spread = cum[:, head : head + 1] - cum_t_ref[head : head + 1, :]
    return jnp.where(mask, jnp.exp(jnp.minimum(spread, 0.0)), 0.0)


def pair_keep(entry, pair):
    row = lax.broadcasted_iota(jnp.int32, (2 * MP, NS), 0)
    last = entry[SPAN - 1 : SPAN, :]
    return jnp.where(
        row < MP, last[:, 2 * pair : 2 * pair + 1], last[:, 2 * pair + 1 : 2 * pair + 2]
    )


def outer_kernel(pairs, v_ref, w_ref, m_ref, out_ref):
    weights = w_ref[...]
    other = m_ref[...]
    for pair in range(pairs):
        block = v_ref[:, pair * 2 * MP : (pair + 1) * 2 * MP]
        block = (block * pair_lanes(weights, pair, block.shape)).astype(jnp.bfloat16)
        out_ref[pair * 2 * MP : (pair + 1) * 2 * MP, :] = contract_rows(block, other)


def weighted_outer(values, weights, other):
    return pl.pallas_call(
        partial(outer_kernel, values.shape[1] // (2 * MP)),
        out_shape=jax.ShapeDtypeStruct((values.shape[1], other.shape[1]), jnp.float32),
        compiler_params=pltpu.CompilerParams(vmem_limit_bytes=VMEM_BYTES),
        name="weighted_outer",
    )(values, weights, other)


def ssm_fwd_kernel(
    pairs,
    x_ref, b_ref, c_ref, step_ref, cum_ref, cum_t_ref, entry_ref, ending_ref, segc_ref, segr_ref,
    init_ref, y_ref, start_ref, state_ref,
):
    @pl.when(pl.program_id(0) == 0)
    def _():
        state_ref[...] = init_ref[...]

    start_ref[0] = state_ref[...]
    b_part, c_part = b_ref[...], c_ref[...]
    steps, cum, entry, ending = step_ref[...], cum_ref[...], entry_ref[...], ending_ref[...]
    mask = span_mask(segc_ref, segr_ref)
    meet = contract_cols(c_part, b_part)
    for pair in range(pairs):
        lanes = slice(pair * 2 * MP, (pair + 1) * 2 * MP)
        shape = (SPAN, 2 * MP)
        inflow = x_ref[:, lanes] * pair_lanes(steps, pair, shape)
        weights = jnp.concatenate(
            [meet * head_decay(mask, cum, cum_t_ref, 2 * pair + k) for k in range(2)], axis=1
        ).astype(jnp.bfloat16)
        state = state_ref[lanes, :]
        y_ref[:, lanes] = dot_nn(weights, split_pair(inflow.astype(jnp.bfloat16))) + pair_lanes(
            entry, pair, shape
        ) * contract_cols(c_part, state.astype(jnp.bfloat16))
        late = (inflow * pair_lanes(ending, pair, shape)).astype(jnp.bfloat16)
        state_ref[lanes, :] = pair_keep(entry, pair) * state + contract_rows(late, b_part)


def ssm_bwd_kernel(
    pairs,
    x_ref, b_ref, c_ref, step_ref, cum_ref, cum_t_ref, entry_ref, ending_ref, segc_ref, segr_ref,
    init_ref, y_ref, start_ref, dy_ref, skip_ref,
    dx_ref, db_ref, dc_ref, dcum_ref, dstep_ref, state_ref,
):
    @pl.when(pl.program_id(0) == 0)
    def _():
        state_ref[...] = init_ref[...]

    b_part, c_part = b_ref[...], c_ref[...]
    steps, cum, entry, ending = step_ref[...], cum_ref[...], entry_ref[...], ending_ref[...]
    mask = span_mask(segc_ref, segr_ref)
    meet = contract_cols(c_part, b_part)
    d_meet = jnp.zeros((SPAN, SPAN), jnp.float32)
    d_b = jnp.zeros((SPAN, NS), jnp.float32)
    d_c = jnp.zeros((SPAN, NS), jnp.float32)
    lane = lax.broadcasted_iota(jnp.int32, (SPAN, 2 * MP), 1)
    token = lax.broadcasted_iota(jnp.int32, (SPAN, 1), 0)
    for pair in range(pairs):
        lanes = slice(pair * 2 * MP, (pair + 1) * 2 * MP)
        shape = (SPAN, 2 * MP)
        x = x_ref[:, lanes]
        step_lanes = pair_lanes(steps, pair, shape)
        end_lanes = pair_lanes(ending, pair, shape)
        inflow = x * step_lanes
        inflow_low = inflow.astype(jnp.bfloat16)
        dy = dy_ref[:, lanes]
        dy_low = dy.astype(jnp.bfloat16)
        dy_split = split_pair(dy_low)
        decays = jnp.concatenate(
            [head_decay(mask, cum, cum_t_ref, 2 * pair + k) for k in range(2)], axis=0
        )
        weights = (jnp.concatenate([meet, meet], axis=0) * decays).astype(jnp.bfloat16)
        grown = contract_cols(dy_split, inflow_low) * decays
        d_meet = d_meet + grown[:SPAN] + grown[SPAN:]
        d_state = state_ref[lanes, :]
        d_state_low = d_state.astype(jnp.bfloat16)
        start = start_ref[0, lanes, :]
        from_end = end_lanes * contract_cols(b_part, d_state_low)
        d_inflow = contract_rows(weights, dy_split) + from_end
        late = (inflow * end_lanes).astype(jnp.bfloat16)
        d_b = d_b + dot_nn(late, d_state_low)
        early = (dy * pair_lanes(entry, pair, shape)).astype(jnp.bfloat16)
        d_c = d_c + dot_nn(early, start.astype(jnp.bfloat16))
        keep = pair_keep(entry, pair)
        kept = keep * d_state * start
        state_ref[lanes, :] = keep * d_state + contract_rows(early, c_part)
        inflow_wide = inflow_low.astype(jnp.float32)
        balance = dy_low.astype(jnp.float32) * y_ref[:, lanes] - inflow_wide * d_inflow
        ended = inflow_wide * from_end
        direct = x * d_inflow
        for k in range(2):
            own = (lane < MP) if k == 0 else (lane >= MP)
            head = 2 * pair + k
            total = jnp.sum(
                jnp.sum(jnp.where(own, ended, 0.0), axis=1, keepdims=True), axis=0, keepdims=True
            ) + jnp.sum(
                jnp.sum(kept[k * MP : (k + 1) * MP], axis=1, keepdims=True), axis=0, keepdims=True
            )
            column = jnp.sum(jnp.where(own, balance, 0.0), axis=1, keepdims=True)
            dcum_ref[:, head : head + 1] = column + jnp.where(token == SPAN - 1, total, 0.0)
            dstep_ref[:, head : head + 1] = jnp.sum(
                jnp.where(own, direct, 0.0), axis=1, keepdims=True
            )
        dx_ref[:, lanes] = step_lanes * d_inflow + skip_ref[:, lanes] * dy
    d_meet_low = d_meet.astype(jnp.bfloat16)
    dc_ref[...] = d_c + dot_nn(d_meet_low, b_part)
    db_ref[...] = d_b + contract_rows(d_meet_low, c_part)


def ssm_specs(count, inner, heads, backward):
    spans = count // SPAN

    def at(i):
        return spans - 1 - i if backward else i

    wide = pl.BlockSpec((SPAN, inner), lambda i: (at(i), 0))
    narrow = pl.BlockSpec((SPAN, NS), lambda i: (at(i), 0))
    per_head = pl.BlockSpec((SPAN, heads), lambda i: (at(i), 0))
    turned = pl.BlockSpec((heads, SPAN), lambda i: (0, at(i)))
    seg_col = pl.BlockSpec((SPAN, 1), lambda i: (at(i), 0))
    seg_row = pl.BlockSpec((1, SPAN), lambda i: (0, at(i)))
    whole = pl.BlockSpec((inner, NS), lambda i: (0, 0))
    starts = pl.BlockSpec((1, inner, NS), lambda i: (at(i), 0, 0))
    flat = pl.BlockSpec((1, inner), lambda i: (0, 0))
    inputs = [wide, narrow, narrow, per_head, per_head, turned, per_head, per_head]
    inputs += [seg_col, seg_row, whole]
    return inputs, wide, narrow, per_head, starts, flat


def ssm_forward(operands, state_in):
    count, inner = operands[0].shape
    heads = operands[3].shape[1]
    inputs, wide, narrow, per_head, starts, flat = ssm_specs(count, inner, heads, False)
    return pl.pallas_call(
        partial(ssm_fwd_kernel, heads // 2),
        grid=(count // SPAN,),
        in_specs=inputs,
        out_specs=[wide, starts],
        out_shape=[
            jax.ShapeDtypeStruct((count, inner), jnp.float32),
            jax.ShapeDtypeStruct((count // SPAN, inner, NS), jnp.float32),
        ],
        scratch_shapes=[pltpu.VMEM((inner, NS), jnp.float32)],
        compiler_params=pltpu.CompilerParams(vmem_limit_bytes=VMEM_BYTES),
        name="ssm_forward",
    )(*operands, state_in)


def ssm_backward(operands, state_grad, y, starting, dy, skip):
    count, inner = operands[0].shape
    heads = operands[3].shape[1]
    inputs, wide, narrow, per_head, starts, flat = ssm_specs(count, inner, heads, True)
    return pl.pallas_call(
        partial(ssm_bwd_kernel, heads // 2),
        grid=(count // SPAN,),
        in_specs=inputs + [wide, starts, wide, flat],
        out_specs=[wide, narrow, narrow, per_head, per_head],
        out_shape=[
            jax.ShapeDtypeStruct((count, inner), jnp.float32),
            jax.ShapeDtypeStruct((count, NS), jnp.float32),
            jax.ShapeDtypeStruct((count, NS), jnp.float32),
            jax.ShapeDtypeStruct((count, heads), jnp.float32),
            jax.ShapeDtypeStruct((count, heads), jnp.float32),
        ],
        scratch_shapes=[pltpu.VMEM((inner, NS), jnp.float32)],
        compiler_params=pltpu.CompilerParams(vmem_limit_bytes=VMEM_BYTES),
        name="ssm_backward",
    )(*operands, state_grad, y, starting, dy, skip)


def span_cumulative(values):
    count, heads = values.shape
    index = jnp.arange(SPAN)
    lower = (index[:, None] >= index[None, :]).astype(jnp.float32)
    spans = values.reshape(count // SPAN, SPAN, heads)
    return jnp.einsum("tu,cuh->cth", lower, spans, precision=HIGHEST).reshape(count, heads)


def span_reverse_cumulative(values):
    count, heads = values.shape
    index = jnp.arange(SPAN)
    upper = (index[:, None] <= index[None, :]).astype(jnp.float32)
    spans = values.reshape(count // SPAN, SPAN, heads)
    return jnp.einsum("tu,cuh->cth", upper, spans, precision=HIGHEST).reshape(count, heads)


def decay_tables(steps, decay_log, seg_local, seg_before):
    count, heads = steps.shape
    spans = count // SPAN
    cum = span_cumulative(steps * (-jnp.exp(decay_log))[None, :])
    by_span = cum.reshape(spans, SPAN, heads)
    seg_spans = seg_local.reshape(spans, SPAN)
    seg_last = seg_spans[:, -1]
    seg_prev = jnp.concatenate([seg_before[None], seg_last[:-1]])
    totals = by_span[:, -1]
    entry = jnp.where((seg_spans == seg_prev[:, None])[..., None], jnp.exp(by_span), 0.0)
    ending = jnp.where(
        (seg_spans == seg_last[:, None])[..., None], jnp.exp(totals[:, None] - by_span), 0.0
    )
    sums = [jnp.zeros_like(totals[0])]
    for span in range(spans):
        sums.append(sums[-1] + totals[span])
    whole = (jnp.stack(sums[:-1])[:, None] + by_span).reshape(count, heads)
    grand = sums[-1]
    seg_end = seg_local[-1]
    entry_all = jnp.where((seg_local == seg_before)[:, None], jnp.exp(whole), 0.0)
    ending_all = jnp.where((seg_local == seg_end)[:, None], jnp.exp(grand[None] - whole), 0.0)
    through = jnp.where(seg_end == seg_before, jnp.exp(grand), 0.0)
    return (
        cum,
        entry.reshape(count, heads),
        ending.reshape(count, heads),
        entry_all,
        ending_all,
        through,
    )


def earlier_states(states, through):
    payload = jnp.concatenate([states, through], axis=0).astype(jnp.bfloat16)
    inner, heads = states.shape[0], states.shape[0] // MP
    total = jnp.zeros(states.shape, jnp.float32)
    factor = jnp.ones((heads,), jnp.float32)
    for step in range(1, lax.axis_size("ctx")):
        got = shifted(payload, step)
        total = total + jnp.repeat(factor, MP)[:, None] * got[:inner].astype(jnp.float32)
        factor = factor * got[inner, :heads].astype(jnp.float32)
    return total


def later_states(d_states, through):
    payload = jnp.concatenate([d_states, through], axis=0).astype(jnp.bfloat16)
    inner, heads = d_states.shape[0], d_states.shape[0] // MP
    total = jnp.zeros(d_states.shape, jnp.float32)
    factor = jnp.ones((heads,), jnp.float32)
    for step in range(1, lax.axis_size("ctx")):
        got = shifted(payload, -step)
        total = total + jnp.repeat(factor, MP)[:, None] * got[:inner].astype(jnp.float32)
        factor = factor * got[inner, :heads].astype(jnp.float32)
    return total


def local(
    tokens, segment, gain_attn, w_query, key_value_weight, w_attn_out, w_gate_z, w_ssm_in, w_step,
    w_bc, w_conv_x, conv_x_bias, w_conv_bc, conv_bc_bias, step_bias, decay_log, skip_gain,
    w_ssm_out, gain_ffn, w_gate, w_up, w_down, grad_out,
):
    qn, kn = w_query.shape[1], key_value_weight.shape[1]
    zn, xn, bn, sn = w_gate_z.shape[1], w_ssm_in.shape[1], w_bc.shape[1], w_step.shape[1]
    fn = w_gate.shape[1]
    an = w_attn_out.shape[0]
    q0, k0, z0, x0 = 0, qn, qn + kn, qn + kn + zn
    b0 = x0 + xn
    s0 = b0 + bn
    g0 = s0 + sn
    first_pack = jnp.concatenate(
        [w_query, key_value_weight, w_gate_z, w_ssm_in, w_bc, w_step]
        + [gain_attn[:, None], gain_ffn[:, None]],
        axis=1,
    )
    out_pack = jnp.concatenate([w_attn_out, w_ssm_out], axis=0).T
    ffn_pack = jnp.concatenate([w_gate, w_up], axis=1)
    full_first = gather_rows(first_pack, "shard")
    full_first, out_pack, ffn_pack, down_pack = lax.optimization_barrier(
        (full_first, out_pack, ffn_pack, w_down.T)
    )
    full_out = gather_rows(out_pack, "shard")
    full_ffn = lax.all_gather(ffn_pack, "shard", axis=0, tiled=True)
    full_down = lax.all_gather(down_pack, "shard", axis=0, tiled=True)

    row_count = tokens.shape[0]
    ctx_rank = lax.axis_index("ctx")
    ctx_count = lax.axis_size("ctx")
    first_row = ctx_rank * row_count
    seg_local = lax.dynamic_slice_in_dim(segment, first_row, row_count)
    seg_before = jnp.where(
        ctx_rank > 0, lax.dynamic_slice_in_dim(segment, jnp.maximum(first_row - 1, 0), 1)[0], -1
    )
    reach = TAPS - 1
    positions = lax.dynamic_slice_in_dim(positions_in_group(segment), first_row, row_count)
    cos_q, sin_q = rope_tables(positions, qn)
    cosine, sine = cos_q[:, :HEAD_SIZE], sin_q[:, :HEAD_SIZE]
    high = (first_row + jnp.arange(row_count, dtype=jnp.int32))[:, None]
    low = high - positions[:, None]
    seg_padded = jnp.concatenate([jnp.full((reach,), -1, jnp.int32), segment])
    seg_ext = lax.dynamic_slice_in_dim(seg_padded, first_row, row_count + reach)
    hidden_in = tokens.astype(jnp.float32)
    gains = full_first[:, g0:].astype(jnp.float32).T
    gain_one, gain_two = gains[0], gains[1]
    scale_one = rms_scale(hidden_in)
    normalized_input = (hidden_in * scale_one * gain_one[None, :]).astype(jnp.bfloat16)
    proj = jnp.dot(normalized_input, full_first, preferred_element_type=jnp.float32)
    queries = rotate(proj[:, q0:k0], cos_q, sin_q).astype(jnp.bfloat16)
    keyval_raw = proj[:, k0:z0]
    keyval = jnp.concatenate(
        [rotate(keyval_raw[:, :HEAD_SIZE], cosine, sine), keyval_raw[:, HEAD_SIZE:]], axis=-1
    ).astype(jnp.bfloat16)
    raw_x = proj[:, x0:b0].astype(jnp.bfloat16)
    raw_bc = proj[:, b0:s0].astype(jnp.bfloat16)
    gate_z = proj[:, z0:x0]
    step_raw = proj[:, s0:g0]
    onward = [(k, k + 1) for k in range(ctx_count - 1)]
    backward = [(k + 1, k) for k in range(ctx_count - 1)]
    tails = lax.ppermute(
        jnp.concatenate([raw_x[row_count - reach :], raw_bc[row_count - reach :]], axis=1),
        "ctx",
        onward,
    )
    all_keys = jnp.zeros((ctx_count * row_count, keyval.shape[1]), keyval.dtype)
    all_keys = lax.dynamic_update_slice_in_dim(all_keys, keyval, first_row, 0)
    for step in range(1, ctx_count):
        all_keys = lax.dynamic_update_slice_in_dim(
            all_keys, shifted(keyval, step), place_from(step) * row_count, 0
        )

    ext_x = jnp.concatenate([tails[:, :xn], raw_x], axis=0).astype(jnp.float32)
    ext_bc = jnp.concatenate([tails[:, xn:], raw_bc], axis=0).astype(jnp.float32)
    conv_x, conv_x_back = jax.vjp(
        lambda extended, taps, bias: conv_silu(extended, taps, bias, seg_ext),
        ext_x,
        w_conv_x,
        conv_x_bias,
    )
    conv_bc, conv_bc_back = jax.vjp(
        lambda extended, taps, bias: conv_silu(extended, taps, bias, seg_ext),
        ext_bc,
        w_conv_bc,
        conv_bc_bias,
    )
    steps = jax.nn.softplus(step_raw + step_bias[None, :])
    mamba_local = step_bias.shape[0]
    b_low = conv_bc[:, :NS].astype(jnp.bfloat16)
    c_low = conv_bc[:, NS:].astype(jnp.bfloat16)
    cum, entry, ending, entry_all, ending_all, through = decay_tables(
        steps, decay_log, seg_local, seg_before
    )
    local_state = weighted_outer(conv_x, steps * ending_all, b_low)
    through_row = jnp.zeros((16, NS), jnp.float32).at[0, :mamba_local].set(through)
    state_in = earlier_states(local_state, through_row)
    attn_out, lse = attn_forward(queries, all_keys, low, high)
    attended = attn_out.astype(jnp.bfloat16)
    operands = (
        conv_x, b_low, c_low, steps, cum, cum.T, entry, ending, seg_local[:, None],
        seg_local[None, :],
    )
    skip_row = jnp.repeat(skip_gain, MP)[None, :]
    y_scan, starting = ssm_forward(operands, state_in)
    scanned = y_scan + skip_row * conv_x
    silu_gate = jax.nn.silu(gate_z)
    gated = (scanned * silu_gate).astype(jnp.bfloat16)
    mixer = jnp.concatenate([attended, gated], axis=1)
    middle = hidden_in + tp_sum(contract_cols(mixer, full_out))

    scale_two = rms_scale(middle)
    normed_ffn = (middle * scale_two * gain_two[None, :]).astype(jnp.bfloat16)
    gate_up = jnp.dot(normed_ffn, full_ffn, preferred_element_type=jnp.float32)
    gate_value, up_value = gate_up[:, :fn], gate_up[:, fn:]
    active = (jax.nn.silu(gate_value) * up_value).astype(jnp.bfloat16)
    d_active = (
        jnp.dot(grad_out, full_down, preferred_element_type=jnp.float32)
        .astype(jnp.bfloat16)
        .astype(jnp.float32)
    )
    d_gate_up = jnp.concatenate(
        [
            (d_active * up_value * silu_slope(gate_value)).astype(jnp.bfloat16),
            (d_active * jax.nn.silu(gate_value)).astype(jnp.bfloat16),
        ],
        axis=1,
    )
    d_normed_ffn = tp_sum(contract_cols(d_gate_up, full_ffn))
    down_part = contract_cols(active, full_down)
    result = (middle + tp_sum(down_part)).astype(jnp.bfloat16)
    grad_down_t = contract_rows(grad_out, active)
    grad_ffn = contract_rows(normed_ffn, d_gate_up)

    def scatter(values, after):
        part = reduce_rows(values, "shard")
        if after is not None:
            part, after = lax.optimization_barrier((part, after))
        return lax.psum(part, "ctx")

    sum_ffn = scatter(
        jnp.concatenate([grad_ffn.astype(jnp.bfloat16), grad_down_t.astype(jnp.bfloat16)], axis=1),
        None,
    )

    d_from_ffn, grad_gain_two = norm_back(middle, scale_two, gain_two, d_normed_ffn)
    d_middle = grad_out.astype(jnp.float32) + d_from_ffn
    d_mid_low = d_middle.astype(jnp.bfloat16)
    d_mixer = jnp.dot(d_mid_low, full_out, preferred_element_type=jnp.float32).astype(jnp.bfloat16)
    d_attended = d_mixer[:, :an]
    d_gated = d_mixer[:, an:].astype(jnp.float32)
    d_scanned = d_gated * silu_gate
    d_gate_z = (d_gated * scanned * silu_slope(gate_z)).astype(jnp.bfloat16)
    grad_skip = jnp.sum((d_scanned * conv_x).reshape(row_count, mamba_local, MP), axis=(0, 2))
    d_state_local = weighted_outer(d_scanned, entry_all, c_low)
    state_grad = later_states(d_state_local, through_row)
    d_query, d_kv_group = attn_backward(queries, all_keys, low, high, attn_out, lse, d_attended)
    d_kv_back = lax.dynamic_slice_in_dim(d_kv_group, first_row, row_count)
    for step in range(1, ctx_count):
        part = lax.dynamic_slice_in_dim(d_kv_group, place_from(step) * row_count, row_count)
        d_kv_back = d_kv_back + shifted(part.astype(jnp.bfloat16), -step).astype(jnp.float32)
    sum_out = scatter(contract_rows(d_mid_low, mixer).astype(jnp.bfloat16), sum_ffn)
    d_keyval = jnp.concatenate(
        [rotate(d_kv_back[:, :HEAD_SIZE], cosine, -sine), d_kv_back[:, HEAD_SIZE:]], axis=-1
    ).astype(jnp.bfloat16)
    d_queries = rotate(d_query, cos_q, -sin_q).astype(jnp.bfloat16)
    d_early = jnp.concatenate([d_queries, d_keyval, d_gate_z], axis=1)
    sum_early = scatter(contract_rows(normalized_input, d_early).astype(jnp.bfloat16), sum_out)
    d_x_post, d_b, d_c, d_cum, d_direct = ssm_backward(
        operands, state_grad, y_scan, starting, d_scanned, skip_row
    )
    d_log = span_reverse_cumulative(d_cum)
    rates = -jnp.exp(decay_log)[None, :]
    grad_decay = jnp.sum(d_log * steps * rates, axis=0)
    d_steps = d_log * rates + d_direct
    d_bc_post = jnp.concatenate([d_b, d_c], axis=-1)
    d_ext_x, grad_convx_taps, grad_convx_bias = conv_x_back(d_x_post)
    d_ext_bc, grad_convbc_taps, grad_convbc_bias = conv_bc_back(d_bc_post)
    d_pre = d_steps * jax.nn.sigmoid(step_raw + step_bias[None, :])
    grad_bias = jnp.sum(d_pre, axis=0)
    back_tails = lax.ppermute(
        jnp.concatenate([d_ext_x[:reach], d_ext_bc[:reach]], axis=1).astype(jnp.bfloat16),
        "ctx",
        backward,
    ).astype(jnp.float32)
    last = row_count - reach
    d_raw_x = d_ext_x[reach:].at[last:].add(back_tails[:, :xn]).astype(jnp.bfloat16)
    d_bc_part = d_ext_bc[reach:].at[last:].add(back_tails[:, xn:]).astype(jnp.bfloat16)
    d_bc_other = lax.ppermute(d_bc_part, "tp", [(0, 1), (1, 0)])
    d_bc = (d_bc_part.astype(jnp.float32) + d_bc_other.astype(jnp.float32)).astype(jnp.bfloat16)
    d_steps_low = d_pre.astype(jnp.bfloat16)
    d_late = jnp.concatenate(
        [d_raw_x, d_bc_part, d_steps_low, jnp.zeros((row_count, 2), jnp.bfloat16)], axis=1
    )
    d_normed = tp_sum(
        contract_cols(d_early, full_first[:, :x0]) + contract_cols(d_late, full_first[:, x0:])
    )
    d_late_sum = jnp.concatenate([d_raw_x, d_bc, d_steps_low], axis=1)
    sum_late = scatter(contract_rows(normalized_input, d_late_sum).astype(jnp.bfloat16), sum_early)
    d_from_attn, grad_gain_one = norm_back(hidden_in, scale_one, gain_one, d_normed)
    grad_tokens = (d_middle + d_from_attn).astype(jnp.bfloat16)

    scalars = jnp.concatenate([grad_bias, grad_decay, grad_skip])
    gain_grads = jnp.concatenate([grad_gain_one, grad_gain_two])
    own = jnp.concatenate(
        [
            grad_convx_taps.reshape(-1),
            grad_convx_bias,
            jnp.pad(scalars, (0, 128 - scalars.shape[0])),
            gain_grads,
            grad_convbc_taps.reshape(-1),
            grad_convbc_bias,
        ]
    ).reshape(-1, 128)
    own = sum_over(own, ("shard", "ctx")).reshape(-1)
    taps_sum = own[: (TAPS + 1) * xn].reshape(TAPS + 1, xn)
    heads_sum = own[(TAPS + 1) * xn : (TAPS + 1) * xn + 128]
    shared = own[(TAPS + 1) * xn + 128 :]
    gain_sums = shared[: gain_grads.shape[0]].reshape(2, -1)
    convbc_sum = sum_over(shared[gain_grads.shape[0] :].reshape(-1, 128), ("tp",))
    convbc_sum = convbc_sum.reshape(TAPS + 1, bn)
    gain_rows = gain_attn.shape[0]
    gain_sums = lax.dynamic_slice_in_dim(
        gain_sums, lax.axis_index("shard") * gain_rows, gain_rows, 1
    )
    sum_ffn, sum_out = sum_ffn.astype(jnp.float32), sum_out.astype(jnp.float32)
    sum_early, sum_late = sum_early.astype(jnp.float32), sum_late.astype(jnp.float32)
    out_t = sum_out.T
    return (
        result,
        grad_tokens,
        gain_sums[0],
        sum_early[:, q0:k0],
        sum_early[:, k0:z0],
        out_t[:an],
        sum_early[:, z0:x0],
        sum_late[:, : b0 - x0],
        sum_late[:, s0 - x0 :],
        sum_late[:, b0 - x0 : s0 - x0],
        taps_sum[:TAPS],
        taps_sum[TAPS],
        convbc_sum[:TAPS],
        convbc_sum[TAPS],
        heads_sum[:mamba_local],
        heads_sum[mamba_local : 2 * mamba_local],
        heads_sum[2 * mamba_local : 3 * mamba_local],
        out_t[an:],
        gain_sums[1],
        sum_ffn[:, :fn],
        sum_ffn[:, fn : 2 * fn],
        sum_ffn[:, 2 * fn :].T,
    )


def solution(mesh):
    return jax.shard_map(
        local,
        mesh=mesh,
        in_specs=(
            P(("shard", "ctx"), None),
            P("shard"),
            P("shard"),
            P("shard", "tp"),
            P("shard", "tp"),
            P("tp", "shard"),
            P("shard", "tp"),
            P("shard", "tp"),
            P("shard", "tp"),
            P("shard", None),
            P(None, "tp"),
            P("tp"),
            P(),
            P(),
            P("tp"),
            P("tp"),
            P("tp"),
            P("tp", "shard"),
            P("shard"),
            P("shard", "tp"),
            P("shard", "tp"),
            P("tp", "shard"),
            P(("shard", "ctx"), None),
        ),
        out_specs=(
            P(("shard", "ctx"), None),
            P(("shard", "ctx"), None),
            P("shard"),
            P("shard", "tp"),
            P("shard", "tp"),
            P("tp", "shard"),
            P("shard", "tp"),
            P("shard", "tp"),
            P("shard", "tp"),
            P("shard", None),
            P(None, "tp"),
            P("tp"),
            P(),
            P(),
            P("tp"),
            P("tp"),
            P("tp"),
            P("tp", "shard"),
            P("shard"),
            P("shard", "tp"),
            P("shard", "tp"),
            P("tp", "shard"),
        ),
        check_vma=False,
    )
```
